32 devices in a mesh: shot: 4 (over y, core), cmp: 8 (over z, x).
Axes of the slice: x: 2, y: 2, z: 4, core: 2. Of those that a mesh axis runs over, the one named last changes fastest.
Arguments:
- traces: float32 [8192, 1024], P(('shot', 'cmp')), may hold values from -6 to 6
- offsets: int32 [8192], P(('shot', 'cmp')), may hold values from 0 to 64
- cmp_bin: int32 [8192, 1], P(('shot', 'cmp')), may hold values from 0 to 255; in each aligned block of 256 rows (0 to 255, 256 to 511, ...) at most 2 rows name the same one
- shot_slot: int32 [8192], P(('shot', 'cmp')), may hold values from 0 to 7
- receiver_id: int32 [8192], P(('shot', 'cmp')), may hold values from 0 to 511
- band: float32 [8, 1024], replicated, may hold values from -2 to 2
Outputs:
- shot_corr: float32 [256, 128], P(('shot', 'cmp'))
- recv_corr: float32 [512, 128], P(('shot', 'cmp'))
The draws below stay inside these ranges and needn't reach their ends.
Inputs may be any that keep to these rules, and one draw needn't show every extreme that they name: `cmp_bin`: among the rows of one device, no bin is named more than 2 times, a bound that some block reaches; every bin is named by some trace.
All inputs are finite; a program needn't handle non-finite values.
Results may differ from the reference program's by a relative error of at most 0.000068.
Values sent between devices are 32-bit elements; how exact they have to be, the bound alone decides.
A program may use at most 64 MiB of HBM per device.

```python
import math
import jax
import jax.numpy as jnp
import numpy as np
from jax import lax

NS = 1024
LAGS = 128
NB = 8
MAXOFF = 64
SLOT = 2
SHOT_DEV = 8
TR_DEV = 256
BINS = 256
TRACES = 8192
SHOTS = 256
RECVS = 512
N_SHOT = 4
N_CMP = 8


def with_ends(array, own_key, least, high):
    extent = array.shape
    index_at = [jax.random.randint(jax.random.fold_in(own_key, axis), (), 0, extent[axis]) for axis in range(len(extent))]
    array = array.at[tuple(index_at)].set(least)
    longest = extent.index(max(extent))
    index_at[longest] = (index_at[longest] + 1) % extent[longest]
    return array.at[tuple(index_at)].set(high)


def steps_of(rng, shape, shards, least, largest):
    factor_of = 1.0
    for position, blocks in shards:
        steps = jax.random.uniform(jax.random.fold_in(jax.random.fold_in(rng, 6), position), (blocks,), jnp.float32, least / len(shards), largest / len(shards))
        factor_of = factor_of * jnp.repeat(jnp.exp(steps), shape[position] // blocks).reshape((-1,) + (1,) * (len(shape) - 1 - position))
    return factor_of


def deal_out(key, own, number, rows, amount, top, reach, lean):
    ranking = jax.random.permutation(key, amount)
    heavy_load, common = portions_of(amount, rows * top, reach, lean, True), portions_of(amount, rows * top, reach, lean, False)
    places = jnp.arange(amount)

    def named(sizes, turn):
        used = int((sizes > 0).sum())
        fixed = max(1, used // 4)
        shifted = fixed + (places - fixed + turn * (used - fixed)) % max(1, amount - fixed)
        return jnp.zeros((amount,), jnp.int32).at[ranking[jnp.where(places < fixed, places, shifted)]].set(jnp.asarray(sizes, jnp.int32))

    sizes = jnp.where(number % 4 == 0, named(heavy_load, number // 4), named(common, number - number // 4 - 1))
    mixed = jax.random.permutation(jax.random.fold_in(own, 3), amount)
    donor, sink = mixed[0:amount // 2 * 2:2], mixed[1:amount // 2 * 2:2]
    slack = jnp.minimum(sizes[donor] - 1, reach - sizes[sink]) // 2
    slack = jnp.where((donor == ranking[0]) | (sink == ranking[0]) | (sizes[sink] == 0), 0, jnp.maximum(slack, 0))
    shifted = jax.random.randint(jax.random.fold_in(own, 4), (amount // 2,), 0, 1 << 20) % (slack + 1)
    sizes = sizes.at[donor].add(-shifted).at[sink].add(shifted)
    items = jnp.searchsorted(jnp.cumsum(sizes), jnp.arange(rows * top), side="right").astype(jnp.int32)
    grid = items.reshape(top, rows).T
    grid = grid[jax.random.permutation(jax.random.fold_in(own, 1), rows)]
    turn = jax.random.randint(jax.random.fold_in(own, 2), (rows, 1), 0, top)
    return jnp.take_along_axis(grid, (jnp.arange(top)[None, :] + turn) % top, axis=1)


def portions_of(number_of, total, reach, skew, full):
    weights = [(1 << 20) // math.isqrt(grade ** skew) + 1 for grade in range(1, number_of + 1)]
    largest = reach if full else min(reach, max(-(-total // number_of), total * weights[0] // sum(weights)))
    least = 1 if total - largest >= number_of - 1 else 0
    holding, rest = [largest] + [least] * (number_of - 1), total - largest - least * (number_of - 1)
    while rest > 0:
        free = [i for i in range(1, number_of) if holding[i] < largest] or [i for i in range(1, number_of) if holding[i] < reach]
        mass, budget = sum([weights[i] for i in free]), rest
        for i in free:
            more = min(reach - holding[i], max(1, budget * weights[i] // mass), rest)
            holding[i] = holding[i] + more
            rest = rest - more
    return np.array(holding)


def noise(stream_key, dims, scale, most, shards=(), kind=jnp.bfloat16):
    array = jax.random.normal(stream_key, dims, jnp.float32) * scale
    if len(shards) > 0:
        array = steps_of(stream_key, dims, shards, -0.22, 0.18) * array
    return jnp.clip(array, min=-most, max=most).astype(kind)


def setup_inputs(seed: int = 0) -> dict:
    streams_of = jax.random.split(jax.random.key(seed), 7)
    traces = noise(streams_of[0], (TRACES, NS), 1.0, 6.0, ((0, 32),), jnp.float32)
    offsets = with_ends(jax.random.randint(streams_of[1], (TRACES,), 0, MAXOFF + 1), jax.random.fold_in(streams_of[1], 1), 0, MAXOFF).astype(jnp.int32)
    cmp_bin_keys = jax.random.split(jax.random.fold_in(streams_of[2], 1), TRACES // TR_DEV)
    cmp_bin_turns = jax.random.permutation(jax.random.fold_in(streams_of[2], 3), TRACES // TR_DEV)
    cmp_bin = jax.vmap(lambda own, number: deal_out(jax.random.fold_in(streams_of[2], 2), own, number, TR_DEV, BINS, 1, SLOT, 2))(cmp_bin_keys, cmp_bin_turns).reshape((TRACES, 1))
    shot_slot = with_ends(jax.random.randint(streams_of[3], (TRACES,), 0, SHOT_DEV), jax.random.fold_in(streams_of[3], 1), 0, SHOT_DEV - 1).astype(jnp.int32)
    receiver_id = with_ends(jax.random.randint(streams_of[4], (TRACES,), 0, RECVS), jax.random.fold_in(streams_of[4], 1), 0, RECVS - 1).astype(jnp.int32)
    band = noise(streams_of[5], (NB, NS), NB ** -0.5, 2.0, (), jnp.float32)
    return {"traces": traces, "offsets": offsets, "cmp_bin": cmp_bin, "shot_slot": shot_slot, "receiver_id": receiver_id, "band": band}


def moveout(block, shifts, band):
    width = block.shape[1]
    taps = band.shape[0]
    padded = jnp.pad(block, ((0, 0), (0, MAXOFF + taps)))

    def single(signal, shift):
        window = lax.dynamic_slice_in_dim(signal, shift, width + taps)
        total = jnp.zeros((width,), jnp.float32)
        for tap_index in range(taps):
            total = total + band[tap_index] * window[tap_index:tap_index + width]
        return total

    return jax.vmap(single)(padded, shifts)


def reference(traces, offsets, cmp_bin, shot_slot, receiver_id, band):
    devices = N_SHOT * N_CMP
    blocks = traces.reshape(devices, TR_DEV, NS)
    shifts = offsets.reshape(devices, TR_DEV)
    corrected = lax.map(lambda pair: moveout(pair[0], pair[1], band), (blocks, shifts)).reshape(TRACES, NS)
    bins = cmp_bin[:, 0]
    fold = jax.ops.segment_sum(jnp.ones((TRACES,), jnp.float32), bins, BINS)
    pilot = jax.ops.segment_sum(corrected, bins, BINS) / fold[:, None]
    half = LAGS // 2
    padded = jnp.pad(pilot, ((0, 0), (half, LAGS - half)))

    def correlate(pair):
        signals, members = pair
        ahead = padded[members]

        def lagged(lag):
            return jnp.sum(signals * lax.dynamic_slice_in_dim(ahead, lag, NS, 1), axis=1)

        return lax.map(lagged, jnp.arange(LAGS, dtype=jnp.int32)).T

    corr = lax.map(correlate, (corrected.reshape(devices, TR_DEV, NS), bins.reshape(devices, TR_DEV)))
    corr = corr.reshape(TRACES, LAGS) * (1.0 / NS)
    shots = (jnp.arange(TRACES, dtype=jnp.int32) // TR_DEV) * SHOT_DEV + shot_slot
    shot_corr = jax.ops.segment_sum(corr, shots, SHOTS)
    recv_corr = jax.ops.segment_sum(corr, receiver_id, RECVS)
    return shot_corr, recv_corr
```

```python
import functools

import jax
import jax.numpy as jnp
from jax import lax
from jax.experimental import pallas as pl
from jax.experimental.pallas import tpu as pltpu
from jax.sharding import PartitionSpec as P

LAGS = 128
MAXOFF = 64
SHOT_DEV = 8
RECV_DEV = 16
LANES = 128
CORES = 2
MESH = pl.DeviceIdType.MESH
VMEM_BYTES = 48 * 1024 * 1024


def vmem():
    return pl.BlockSpec(memory_space=pltpu.VMEM)


def halves(value):
    high = value.astype(jnp.bfloat16)
    low = (value - high.astype(jnp.float32)).astype(jnp.bfloat16)
    return high, low


def dot2(table, value, dims):
    high, low = halves(value)
    args = dict(dimension_numbers=(dims, ((), ())), preferred_element_type=jnp.float32)
    return lax.dot_general(table, high, **args) + lax.dot_general(table, low, **args)


def moveout_kernel(bins_count, traces_ref, offsets_ref, bins_ref, band_ref, sums_ref, turned_ref, corrected):
    rows, samples = traces_ref.shape
    taps = band_ref.shape[0]
    width = samples + LANES
    group = 32
    shifts = jnp.transpose(jnp.broadcast_to(offsets_ref[...], (LANES, rows)))
    turned_ref[...] = jnp.zeros_like(turned_ref)
    corrected[:, samples:] = jnp.ones((rows, LANES), jnp.float32)
    for start in range(0, rows, group):
        block = slice(start, start + group)
        current = jnp.concatenate([traces_ref[block, :], jnp.zeros((group, LANES), jnp.float32)], axis=1)
        shift = shifts[block, :]
        for level in range(MAXOFF.bit_length()):
            moved = pltpu.roll(current, width - (1 << level), 1)
            chosen = jnp.concatenate([(shift >> level) & 1] * (width // LANES), axis=1) == 1
            current = jnp.where(chosen, moved, current)
        total = jnp.zeros((group, samples), jnp.float32)
        for tap in range(taps):
            moved = current if tap == 0 else pltpu.roll(current, width - tap, 1)
            total = total + band_ref[tap : tap + 1, :] * moved[:, :samples]
        corrected[block, :samples] = total
    table = (
        bins_ref[...] == lax.broadcasted_iota(jnp.int32, (rows, bins_count), 1)
    ).astype(jnp.float32)
    table = jnp.transpose(table).astype(jnp.bfloat16)
    sums_ref[...] = dot2(table, corrected[...], ((1,), (0,)))
    turned_ref[...] = jnp.transpose(corrected[:, :samples])


def moveout(traces, offsets, cmp_bin, band, bins_count):
    rows, samples = traces.shape
    return pl.pallas_call(
        functools.partial(moveout_kernel, bins_count),
        out_shape=(
            jax.ShapeDtypeStruct((bins_count, samples + LANES), jnp.float32),
            jax.ShapeDtypeStruct((samples, rows), jnp.float32),
        ),
        in_specs=[vmem()] * 4,
        out_specs=(vmem(), vmem()),
        scratch_shapes=[pltpu.VMEM((rows, samples + LANES), jnp.float32)],
        compiler_params=pltpu.CompilerParams(vmem_limit_bytes=VMEM_BYTES),
        name="moveout_sums",
    )(traces, offsets[None, :], cmp_bin, band)


def place(sizes):
    y_size, x_size, z_size = sizes
    shot, cmp = lax.axis_index("shot"), lax.axis_index("cmp")
    return shot % CORES, shot // CORES, cmp % x_size, cmp // x_size


def device(sizes, core, y, x, z):
    return (y * CORES + core, z * sizes[1] + x)


def greet(sizes):
    y_size, x_size, z_size = sizes
    core, y, x, z = place(sizes)
    peers = [device(sizes, 1 - core, y, x, z)]
    peers += [device(sizes, core, (y + k) % y_size, x, z) for k in range(1, y_size)]
    peers += [device(sizes, core, y, (x + k) % x_size, z) for k in range(1, x_size)]
    peers += [device(sizes, core, y, x, (z + k) % z_size) for k in range(1, z_size)]
    barrier = pltpu.get_barrier_semaphore()
    for peer in peers:
        pl.semaphore_signal(barrier, inc=1, device_id=peer, device_id_type=MESH)
    pl.semaphore_wait(barrier, len(peers))


class Sender:
    def __init__(self, send_sems, recv_sems):
        self.send_sems, self.recv_sems, self.used = send_sems, recv_sems, 0

    def start(self, source, target, peer):
        copy = pltpu.make_async_remote_copy(
            src_ref=source,
            dst_ref=target,
            send_sem=self.send_sems.at[self.used],
            recv_sem=self.recv_sems.at[self.used],
            device_id=peer,
            device_id_type=MESH,
        )
        self.used += 1
        copy.start()
        return copy


def scatter_sums(sizes, cut, sender, sums, got_core, acc, got_y, got_x, acc_y, acc_x, got_yx, got_xy, acc_z, got_z):
    y_size, x_size, z_size = sizes
    core, y, x, z = place(sizes)
    lo, hi = pl.ds(0, cut), pl.ds(cut, sums.shape[-1] - cut)
    y_peer = lambda k: device(sizes, core, (y + k) % y_size, x, z)
    x_peer = lambda k: device(sizes, core, y, (x + k) % x_size, z)
    z_peer = lambda k: device(sizes, core, y, x, (z + k) % z_size)
    pending = []

    first = sender.start(sums.at[1 - core], got_core, device(sizes, 1 - core, y, x, z))
    pending.append(first)
    first.wait_recv()
    acc[...] = sums[core] + got_core[...]

    ys = [sender.start(acc.at[(y + k) % y_size, :, :, :, lo], got_y.at[k - 1], y_peer(k)) for k in range(1, y_size)]
    xs = [sender.start(acc.at[:, (x + k) % x_size, :, :, hi], got_x.at[k - 1], x_peer(k)) for k in range(1, x_size)]
    pending += ys + xs
    total = acc[y, :, :, :, :cut]
    for k, copy in enumerate(ys):
        copy.wait_recv()
        total = total + got_y[k]
    acc_y[...] = total
    yxs = [sender.start(acc_y.at[(x + k) % x_size], got_yx.at[k - 1], x_peer(k)) for k in range(1, x_size)]
    total = acc[:, x, :, :, cut:]
    for k, copy in enumerate(xs):
        copy.wait_recv()
        total = total + got_x[k]
    acc_x[...] = total
    xys = [sender.start(acc_x.at[(y + k) % y_size], got_xy.at[k - 1], y_peer(k)) for k in range(1, y_size)]
    pending += yxs + xys
    total = acc_y[x]
    for k, copy in enumerate(yxs):
        copy.wait_recv()
        total = total + got_yx[k]
    acc_z[:, :, :cut] = total
    total = acc_x[y]
    for k, copy in enumerate(xys):
        copy.wait_recv()
        total = total + got_xy[k]
    acc_z[:, :, cut:] = total
    zs = [sender.start(acc_z.at[(z + k) % z_size], got_z.at[k - 1], z_peer(k)) for k in range(1, z_size)]
    pending += zs
    total = acc_z[z]
    for k, copy in enumerate(zs):
        copy.wait_recv()
        total = total + got_z[k]
    return total, pending


def scatter_scratch(sizes, rows, width, cut):
    y_size, x_size, z_size = sizes
    shapes = [
        (y_size, x_size, z_size, rows, width),
        (y_size, x_size, z_size, rows, width),
        (y_size - 1, x_size, z_size, rows, cut),
        (x_size - 1, y_size, z_size, rows, width - cut),
        (x_size, z_size, rows, cut),
        (y_size, z_size, rows, width - cut),
        (x_size - 1, z_size, rows, cut),
        (y_size - 1, z_size, rows, width - cut),
        (z_size, rows, width),
        (z_size - 1, rows, width),
    ]
    return [pltpu.VMEM(shape, jnp.float32) for shape in shapes]


def scatter_copies(sizes):
    return 1 + 2 * (sizes[0] - 1) + 2 * (sizes[1] - 1) + sizes[2] - 1


def pilot_kernel(sizes, cut, sums, pilots, send_sems, recv_sems, *scratch):
    y_size, x_size, z_size = sizes
    core, y, x, z = place(sizes)
    samples = pilots.shape[-1]
    greet(sizes)
    sender = Sender(send_sems, recv_sems)
    total, pending = scatter_sums(sizes, cut, sender, sums, *scratch)
    fold = jnp.concatenate([total[:, samples:]] * (samples // LANES), axis=1)
    pilots[core, y, x, z] = total[:, :samples] / fold

    lo, hi = pl.ds(0, cut), pl.ds(cut, samples - cut)
    other = device(sizes, 1 - core, y, x, z)
    y_peer = lambda k: device(sizes, core, (y + k) % y_size, x, z)
    x_peer = lambda k: device(sizes, core, y, (x + k) % x_size, z)

    def send(view, peer):
        return sender.start(view, view, peer)

    zs = [send(pilots.at[core, y, x, z], device(sizes, core, y, x, (z + k) % z_size)) for k in range(1, z_size)]
    for copy in zs:
        copy.wait_recv()
    own_lo, own_hi = pilots.at[core, y, x, :, :, lo], pilots.at[core, y, x, :, :, hi]
    ys = [send(own_lo, y_peer(k)) for k in range(1, y_size)]
    xs = [send(own_hi, x_peer(k)) for k in range(1, x_size)]
    across = [send(pilots.at[core, y, x], other)]
    for copy in ys:
        copy.wait_recv()
    yxs = [send(pilots.at[core, :, x, :, :, lo], x_peer(k)) for k in range(1, x_size)]
    for copy in xs:
        copy.wait_recv()
    xys = [send(pilots.at[core, y, :, :, :, hi], y_peer(k)) for k in range(1, y_size)]
    for k in range(1, y_size):
        across.append(send(pilots.at[core, (y + k) % y_size, x, :, :, lo], other))
    for k in range(1, x_size):
        across.append(send(pilots.at[core, y, (x + k) % x_size, :, :, hi], other))
    for k, copy in enumerate(yxs, 1):
        copy.wait_recv()
        across.append(send(pilots.at[core, :, (x + k) % x_size, :, :, lo], other))
    for k, copy in enumerate(xys, 1):
        copy.wait_recv()
        across.append(send(pilots.at[core, (y + k) % y_size, :, :, :, hi], other))
    for copy in across:
        copy.wait_recv()
    for copy in pending + zs + ys + xs + yxs + xys + across:
        copy.wait_send()


def share_pilots(sums, sizes, samples):
    y_size, x_size, z_size = sizes
    cut = samples // 2
    blocks = (CORES, y_size, x_size, z_size)
    rows = sums.shape[0] // (CORES * y_size * x_size * z_size)
    width = sums.shape[1]
    copies = scatter_copies(sizes) + (z_size - 1) + 4 * (y_size - 1) + 4 * (x_size - 1) + 1
    pilots = pl.pallas_call(
        functools.partial(pilot_kernel, sizes, cut),
        out_shape=jax.ShapeDtypeStruct(blocks + (rows, samples), jnp.float32),
        in_specs=[vmem()],
        out_specs=vmem(),
        scratch_shapes=[pltpu.SemaphoreType.DMA((copies,))] * 2 + scatter_scratch(sizes, rows, width, cut),
        compiler_params=pltpu.CompilerParams(
            collective_id=0, has_side_effects=True, vmem_limit_bytes=VMEM_BYTES
        ),
        name="share_pilots",
    )(sums.reshape(blocks + (rows, width)))
    return pilots.reshape(sums.shape[0], samples)


def correlate_kernel(turned_ref, pilots_ref, bins_ref, slots_ref, receivers_ref, shot_ref, recv_ref, ahead, moved, parts, corr):
    samples, rows = turned_ref.shape
    bins_count = pilots_ref.shape[0]
    half = LAGS // 2
    span = moved.shape[0]
    table = (
        bins_ref[...] == lax.broadcasted_iota(jnp.int32, (rows, bins_count), 1)
    ).astype(jnp.bfloat16)
    gathered = dot2(table, pilots_ref[...], ((1,), (0,)))
    ahead[:half, :] = jnp.zeros((half, rows), jnp.float32)
    ahead[half : half + samples, :] = jnp.transpose(gathered)
    ahead[half + samples :, :] = jnp.zeros((ahead.shape[0] - half - samples, rows), jnp.float32)
    lags = LAGS // 8
    steps = 4
    for residue in range(8):
        source = ahead if residue == 0 else moved
        if residue > 0:
            moved[...] = ahead[residue : residue + span, :]
        for lane in range(0, rows, LANES):
            columns = slice(lane, lane + LANES)

            def step(index, totals):
                base = pl.multiple_of(index * (8 * steps), 8 * steps)
                signal = [turned_ref[pl.ds(base + 8 * k, 8), columns] for k in range(steps)]
                pilot = [source[pl.ds(base + 8 * k, 8), columns] for k in range(lags + steps - 1)]
                totals = list(totals)
                for lag in range(lags):
                    terms = [signal[k] * pilot[k + lag] for k in range(steps)]
                    totals[lag] = totals[lag] + ((terms[0] + terms[1]) + (terms[2] + terms[3]))
                return tuple(totals)

            zero = jnp.zeros((8, LANES), jnp.float32)
            totals = lax.fori_loop(0, samples // (8 * steps), step, (zero,) * lags)
            for lag in range(lags):
                parts[8 * lag + residue, :, columns] = totals[lag]
    corr[...] = jnp.sum(parts[...], axis=1) * (1.0 / samples)
    high, low = halves(corr[...])
    for ids_ref, out_ref in ((slots_ref, shot_ref), (receivers_ref, recv_ref)):
        count = out_ref.shape[0]
        ids = (ids_ref[...] == lax.broadcasted_iota(jnp.int32, (count, rows), 0)).astype(jnp.bfloat16)
        args = dict(dimension_numbers=(((1,), (1,)), ((), ())), preferred_element_type=jnp.float32)
        out_ref[...] = lax.dot_general(ids, high, **args) + lax.dot_general(ids, low, **args)


def correlate(turned, pilots, cmp_bin, shot_slot, receivers, receivers_count):
    samples, rows = turned.shape
    return pl.pallas_call(
        correlate_kernel,
        out_shape=(
            jax.ShapeDtypeStruct((SHOT_DEV, LAGS), jnp.float32),
            jax.ShapeDtypeStruct((receivers_count, LAGS), jnp.float32),
        ),
        in_specs=[vmem()] * 5,
        out_specs=(vmem(), vmem()),
        scratch_shapes=[
            pltpu.VMEM((samples + LAGS, rows), jnp.float32),
            pltpu.VMEM((samples + LAGS - 8, rows), jnp.float32),
            pltpu.VMEM((LAGS, 8, rows), jnp.float32),
            pltpu.VMEM((LAGS, rows), jnp.float32),
        ],
        compiler_params=pltpu.CompilerParams(vmem_limit_bytes=VMEM_BYTES),
        name="correlate_sums",
    )(turned, pilots, cmp_bin, shot_slot[None, :], receivers[None, :])


def local(sizes, bins_count, traces, offsets, cmp_bin, shot_slot, receiver_id, band):
    samples = traces.shape[1]
    devices = lax.axis_size(("shot", "cmp"))
    sums, turned = moveout(traces, offsets, cmp_bin, band, bins_count)
    pilots = share_pilots(sums, sizes, samples)
    shot_corr, partial = correlate(turned, pilots, cmp_bin, shot_slot, receiver_id, RECV_DEV * devices)
    parts = lax.all_to_all(
        partial.reshape(devices, RECV_DEV, LAGS), ("shot", "cmp"), split_axis=0, concat_axis=0, tiled=True
    )
    return shot_corr, jnp.sum(parts, axis=0)


def solution(mesh):
    shot_size, cmp_size = mesh.shape["shot"], mesh.shape["cmp"]
    z_size = 4 if cmp_size % 4 == 0 else 1
    sizes = (shot_size // CORES, cmp_size // z_size, z_size)
    placed = (
        P(("shot", "cmp"), None),
        P(("shot", "cmp")),
        P(("shot", "cmp"), None),
        P(("shot", "cmp")),
        P(("shot", "cmp")),
        P(),
    )

    def whole(traces, offsets, cmp_bin, shot_slot, receiver_id, band):
        bins_count = traces.shape[0] // (shot_size * cmp_size)
        return jax.shard_map(
            functools.partial(local, sizes, bins_count),
            mesh=mesh,
            in_specs=placed,
            out_specs=(P(("shot", "cmp"), None), P(("shot", "cmp"), None)),
            check_vma=False,
        )(traces, offsets, cmp_bin, shot_slot, receiver_id, band)

    return whole
```

```python
import functools

import jax
import jax.numpy as jnp
from jax import lax
from jax.experimental import pallas as pl
from jax.experimental.pallas import tpu as pltpu
from jax.sharding import PartitionSpec as P

LAGS = 128
MAXOFF = 64
SHOT_DEV = 8
RECV_DEV = 16
LANES = 128
CORES = 2
CHUNKS = 4
GROUP = 32
MESH = pl.DeviceIdType.MESH
VMEM_BYTES = 56 * 1024 * 1024


def halves(value):
    high = value.astype(jnp.bfloat16)
    low = (value - high.astype(jnp.float32)).astype(jnp.bfloat16)
    return high, low


def dot2(table, value, dims):
    high, low = halves(value)
    args = dict(dimension_numbers=(dims, ((), ())), preferred_element_type=jnp.float32)
    return lax.dot_general(table, high, **args) + lax.dot_general(table, low, **args)


def log2(size):
    return size.bit_length() - 1


class Sender:
    def __init__(self, send_sems, recv_sems):
        self.send_sems, self.recv_sems, self.copies = send_sems, recv_sems, []

    def start(self, source, target, peer):
        copy = pltpu.make_async_remote_copy(
            src_ref=source,
            dst_ref=target,
            send_sem=self.send_sems.at[len(self.copies)],
            recv_sem=self.recv_sems.at[len(self.copies)],
            device_id=peer,
            device_id_type=MESH,
        )
        self.copies.append(copy)
        copy.start()
        return copy


def copies_count(plane, z_size):
    scatter = 1 + (plane - 1) + (z_size - 1)
    return CHUNKS * (2 * scatter + plane - 1) + scatter


def kernel(
    sizes,
    traces_ref, offsets_ref, bins_ref, slots_ref, receivers_ref, band_ref,
    shot_ref, recv_ref,
    traces, corrected, table_t, table, shifts, padded, moved, ahead, parts, fold,
    sums, got_core, acc, got_plane, acc_z, got_z, pilots,
    rsums, rgot_core, racc, rgot_plane, racc_z, rgot_z,
    load_sems, send_sems, recv_sems,
):
    y_size, x_size, z_size = sizes
    plane = y_size * x_size
    shot, cmp = lax.axis_index("shot"), lax.axis_index("cmp")
    core, y, x, z = shot % CORES, shot // CORES, cmp % x_size, cmp // x_size
    q = y * x_size + x
    rows, samples = traces_ref.shape
    bins_count = rows
    chunk = samples // CHUNKS
    taps = band_ref.shape[0]
    held = sums.shape[-2]
    half = LAGS // 2

    def device(core, q, z):
        return ((q // x_size) * CORES + core, z * x_size + q % x_size)

    other = device(1 - core, q, z)
    plane_peers = [device(core, (q + k) % plane, z) for k in range(1, plane)]
    z_peers = [device(core, q, (z + k) % z_size) for k in range(1, z_size)]

    loads = []
    for k in range(CHUNKS):
        columns = pl.ds(k * chunk, chunk)
        loads.append(pltpu.make_async_copy(traces_ref.at[:, columns], traces.at[:, columns], load_sems.at[k]))
        loads[-1].start()
    barrier = pltpu.get_barrier_semaphore()
    peers = [other] + plane_peers + z_peers
    for peer in peers:
        pl.semaphore_signal(barrier, inc=1, device_id=peer, device_id_type=MESH)

    sender = Sender(send_sems, recv_sems)
    shifts[...] = jnp.transpose(jnp.broadcast_to(offsets_ref[...], (LANES, rows)))
    named = (bins_ref[...] == lax.broadcasted_iota(jnp.int32, (bins_count, rows), 0)).astype(jnp.float32)
    table_t[...] = named.astype(jnp.bfloat16)
    table[...] = jnp.transpose(named).astype(jnp.bfloat16)
    traces[:, samples:] = jnp.zeros((rows, LANES), jnp.float32)
    corrected[:, chunk:] = jnp.ones((rows, LANES), jnp.float32)
    padded[:half, :] = jnp.zeros((half, rows), jnp.float32)
    padded[half + samples :, :] = jnp.zeros((half, rows), jnp.float32)

    def width_of(k):
        return chunk + LANES if k == 0 else chunk

    def correct(k):
        first = k * chunk
        loads[k].wait() if k == 0 else None
        if k + 1 < CHUNKS:
            loads[k + 1].wait()
        span = chunk + LANES

        def group(index, carry):
            block = pl.ds(pl.multiple_of(index * GROUP, GROUP), GROUP)
            current = traces[block, first : first + span]
            shift = shifts[block, :]
            for level in range(MAXOFF.bit_length()):
                turned = pltpu.roll(current, span - (1 << level), 1)
                chosen = jnp.concatenate([(shift >> level) & 1] * (span // LANES), axis=1) == 1
                current = jnp.where(chosen, turned, current)
            total = jnp.zeros((GROUP, chunk), jnp.float32)
            for tap in range(taps):
                turned = current if tap == 0 else pltpu.roll(current, span - tap, 1)
                total = total + band_ref[tap : tap + 1, first : first + chunk] * turned[:, :chunk]
            corrected[block, :chunk] = total
            return carry

        lax.fori_loop(0, rows // GROUP, group, 0)
        width = width_of(k)
        result = dot2(table_t[...], corrected[:, :width], ((1,), (0,)))
        if held % 8 == 0:
            sums[k, :, :, :, :, :width] = result.reshape(CORES, plane, z_size, held, width)
        else:
            for block in range(CORES * plane * z_size):
                c_of, rest = divmod(block, plane * z_size)
                sums[k, c_of, rest // z_size, rest % z_size, :, :width] = result[block * held : (block + 1) * held]
        padded[half + first : half + first + chunk, :] = jnp.transpose(corrected[:, :chunk])

    def scatter_core(k):
        lanes = pl.ds(0, width_of(k))
        return [sender.start(sums.at[k, 1 - core, :, :, :, lanes], got_core.at[k, :, :, :, lanes], other)]

    def scatter_plane(k, waits):
        width = width_of(k)
        lanes = pl.ds(0, width)
        waits[0].wait_recv()
        acc[k, :, :, :, :width] = sums[k, core, :, :, :, :width] + got_core[k, :, :, :, :width]
        return [
            sender.start(acc.at[k, (q + j) % plane, :, :, lanes], got_plane.at[k, j - 1, :, :, lanes], plane_peers[j - 1])
            for j in range(1, plane)
        ]

    def scatter_z(k, waits):
        width = width_of(k)
        lanes = pl.ds(0, width)
        total = acc[k, q, :, :, :width]
        for j, copy in enumerate(waits):
            copy.wait_recv()
            total = total + got_plane[k, j, :, :, :width]
        acc_z[k, :, :, :width] = total
        return [
            sender.start(acc_z.at[k, (z + j) % z_size, :, lanes], got_z.at[k, j - 1, :, lanes], z_peers[j - 1])
            for j in range(1, z_size)
        ]

    def gather_z(k, waits):
        width = width_of(k)
        total = acc_z[k, z, :, :width]
        for j, copy in enumerate(waits):
            copy.wait_recv()
            total = total + got_z[k, j, :, :width]
        if k == 0:
            fold[...] = total[:, chunk:]
        pilots[k, core, q, z] = total[:, :chunk] / jnp.concatenate([fold[...]] * (chunk // LANES), axis=1)
        own = pilots.at[k, core, q, z]
        return [sender.start(own, own, peer) for peer in z_peers]

    def gather_plane(k, waits):
        for copy in waits:
            copy.wait_recv()
        own = pilots.at[k, core, q]
        return [sender.start(own, own, peer) for peer in plane_peers] + [sender.start(own, own, other)]

    def gather_core(k, waits):
        across = [waits[-1]]
        for j, copy in enumerate(waits[:-1], 1):
            copy.wait_recv()
            came = pilots.at[k, core, (q + plane - j) % plane]
            across.append(sender.start(came, came, other))
        return across

    def correlate(k, waits):
        for copy in waits:
            copy.wait_recv()
        if held % 8 == 0:
            pilot = pilots[k].reshape(bins_count, chunk)
        else:
            pilot = jnp.concatenate(
                [
                    pilots[k, n // (plane * z_size), n // z_size % plane, n % z_size]
                    for n in range(CORES * plane * z_size)
                ],
                axis=0,
            )
        ahead[...] = jnp.transpose(dot2(table[...], pilot, ((1,), (0,))))
        lags = LAGS // 8
        steps = 4

        def residue(index, carry):
            for lane in range(0, rows, LANES):
                columns = slice(lane, lane + LANES)

                def step(index_in, totals):
                    base = pl.multiple_of(index_in * (8 * steps), 8 * steps)
                    signal = [ahead[pl.ds(base + 8 * i, 8), columns] for i in range(steps)]
                    shifted = [
                        moved[index, pl.ds(k * chunk + base + 8 * i, 8), columns] for i in range(lags + steps - 1)
                    ]
                    totals = list(totals)
                    for lag in range(lags):
                        terms = [signal[i] * shifted[i + lag] for i in range(steps)]
                        totals[lag] = totals[lag] + ((terms[0] + terms[1]) + (terms[2] + terms[3]))
                    return tuple(totals)

                zero = jnp.zeros((8, LANES), jnp.float32)
                before = tuple(
                    zero if k == 0 else parts[lags - 1 - lag, 7 - index, :, columns] for lag in range(lags)
                )
                totals = lax.fori_loop(0, chunk // (8 * steps), step, before)
                for lag in range(lags):
                    parts[lags - 1 - lag, 7 - index, :, columns] = totals[lag]
            return carry

        lax.fori_loop(0, 8, residue, 0)

    def shift_copies(index):
        moved[index] = padded[index + 1 : index + 1 + moved.shape[1], :]

    stages = [scatter_plane, scatter_z, gather_z, gather_plane, gather_core, correlate]
    waits = [None] * CHUNKS
    fillers = list(range(8))
    for turn in range(CHUNKS + len(stages)):
        if turn < CHUNKS:
            correct(turn)
            if turn == 0:
                pl.semaphore_wait(barrier, len(peers))
            waits[turn] = scatter_core(turn)
        for k in range(CHUNKS):
            stage = turn - k - 1
            if 0 <= stage < len(stages) - 1:
                waits[k] = stages[stage](k, waits[k])
        if turn >= CHUNKS - 1:
            for _ in range(4):
                if fillers:
                    shift_copies(fillers.pop())
        k = turn - len(stages)
        if 0 <= k < CHUNKS:
            while fillers:
                shift_copies(fillers.pop())
            correlate(k, waits[k])

    corr = (jnp.sum(parts[...], axis=2) * (1.0 / samples)).reshape(LAGS, rows)
    high, low = halves(corr)

    def tabled(ids, count):
        args = dict(dimension_numbers=(((1,), (1,)), ((), ())), preferred_element_type=jnp.float32)
        chosen = (ids == lax.broadcasted_iota(jnp.int32, (count, rows), 0)).astype(jnp.bfloat16)
        return lax.dot_general(chosen, high, **args) + lax.dot_general(chosen, low, **args)

    ids = receivers_ref[...]
    within = ids & (RECV_DEV - 1)
    owner = ids >> log2(RECV_DEV)
    owner_x = owner & (x_size - 1)
    owner_z = (owner >> log2(x_size)) & (z_size - 1)
    owner_core = (owner >> log2(x_size * z_size)) & 1
    owner_y = owner >> log2(x_size * z_size * CORES)
    block = ((owner_core * y_size + owner_y) * x_size + owner_x) * z_size + owner_z
    rsums[...] = tabled(block * RECV_DEV + within, CORES * plane * z_size * RECV_DEV).reshape(rsums.shape)
    first = sender.start(rsums.at[1 - core], rgot_core, other)
    shot_ref[...] = tabled(slots_ref[...], SHOT_DEV)
    first.wait_recv()
    racc[...] = rsums[core] + rgot_core[...]
    waiting = [
        sender.start(racc.at[(q + j) % plane], rgot_plane.at[j - 1], plane_peers[j - 1]) for j in range(1, plane)
    ]
    total = racc[q]
    for j, copy in enumerate(waiting):
        copy.wait_recv()
        total = total + rgot_plane[j]
    racc_z[...] = total
    waiting = [
        sender.start(racc_z.at[(z + j) % z_size], rgot_z.at[j - 1], z_peers[j - 1]) for j in range(1, z_size)
    ]
    total = racc_z[z]
    for j, copy in enumerate(waiting):
        copy.wait_recv()
        total = total + rgot_z[j]
    recv_ref[...] = total
    for copy in sender.copies:
        copy.wait_send()


def local(sizes, traces, offsets, cmp_bin, shot_slot, receiver_id, band):
    rows, samples = traces.shape
    y_size, x_size, z_size = sizes
    plane = y_size * x_size
    held = rows // (CORES * plane * z_size)
    chunk = samples // CHUNKS
    wide = chunk + LANES
    copies = copies_count(plane, z_size)

    def buffer(*shape):
        return pltpu.VMEM(shape, jnp.float32)

    vmem = pl.BlockSpec(memory_space=pltpu.VMEM)
    return pl.pallas_call(
        functools.partial(kernel, sizes),
        out_shape=(
            jax.ShapeDtypeStruct((SHOT_DEV, LAGS), jnp.float32),
            jax.ShapeDtypeStruct((RECV_DEV, LAGS), jnp.float32),
        ),
        in_specs=[pl.BlockSpec(memory_space=pl.ANY)] + [vmem] * 5,
        out_specs=(vmem, vmem),
        scratch_shapes=[
            buffer(rows, samples + LANES),
            buffer(rows, wide),
            pltpu.VMEM((rows, rows), jnp.bfloat16),
            pltpu.VMEM((rows, rows), jnp.bfloat16),
            pltpu.VMEM((rows, LANES), jnp.int32),
            buffer(samples + LAGS, rows),
            buffer(8, samples + LAGS - 8, rows),
            buffer(chunk, rows),
            buffer(LAGS // 8, 8, 8, rows),
            buffer(held, LANES),
            buffer(CHUNKS, CORES, plane, z_size, held, wide),
            buffer(CHUNKS, plane, z_size, held, wide),
            buffer(CHUNKS, plane, z_size, held, wide),
            buffer(CHUNKS, plane - 1, z_size, held, wide),
            buffer(CHUNKS, z_size, held, wide),
            buffer(CHUNKS, z_size - 1, held, wide),
            buffer(CHUNKS, CORES, plane, z_size, held, chunk),
            buffer(CORES, plane, z_size, RECV_DEV, LAGS),
            buffer(plane, z_size, RECV_DEV, LAGS),
            buffer(plane, z_size, RECV_DEV, LAGS),
            buffer(plane - 1, z_size, RECV_DEV, LAGS),
            buffer(z_size, RECV_DEV, LAGS),
            buffer(z_size - 1, RECV_DEV, LAGS),
            pltpu.SemaphoreType.DMA((CHUNKS,)),
            pltpu.SemaphoreType.DMA((copies,)),
            pltpu.SemaphoreType.DMA((copies,)),
        ],
        compiler_params=pltpu.CompilerParams(
            collective_id=0, has_side_effects=True, vmem_limit_bytes=VMEM_BYTES
        ),
        name="residual_statics",
    )(
        traces,
        offsets.reshape(1, rows),
        cmp_bin.reshape(1, rows),
        shot_slot.reshape(1, rows),
        receiver_id.reshape(1, rows),
        band,
    )


def solution(mesh):
    shot_size, cmp_size = mesh.shape["shot"], mesh.shape["cmp"]
    z_size = 4 if cmp_size % 8 == 0 else 2
    sizes = (shot_size // CORES, cmp_size // z_size, z_size)
    placed = (
        P(("shot", "cmp"), None),
        P(("shot", "cmp")),
        P(("shot", "cmp"), None),
        P(("shot", "cmp")),
        P(("shot", "cmp")),
        P(),
    )
    return jax.shard_map(
        functools.partial(local, sizes),
        mesh=mesh,
        in_specs=placed,
        out_specs=(P(("shot", "cmp"), None), P(("shot", "cmp"), None)),
        check_vma=False,
    )
```

```python
import functools

import jax
import jax.numpy as jnp
from jax import lax
from jax.experimental import pallas as pl
from jax.experimental.pallas import tpu as pltpu
from jax.sharding import PartitionSpec as P

LAGS = 128
MAXOFF = 64
SHOT_DEV = 8
RECV_DEV = 16
LANES = 128
CORES = 2
CHUNKS = 4
GROUP = 32
UNIT = 1
MESH = pl.DeviceIdType.MESH
VMEM_BYTES = 56 * 1024 * 1024


def halves(value):
    high = value.astype(jnp.bfloat16)
    low = (value - high.astype(jnp.float32)).astype(jnp.bfloat16)
    return high, low


def dot2(table, value, dims):
    high, low = halves(value)
    args = dict(dimension_numbers=(dims, ((), ())), preferred_element_type=jnp.float32)
    return lax.dot_general(table, high, **args) + lax.dot_general(table, low, **args)


def log2(size):
    return size.bit_length() - 1


class Sender:
    def __init__(self, send_sems, recv_sems):
        self.send_sems, self.recv_sems, self.copies = send_sems, recv_sems, []

    def start(self, source, target, peer):
        copy = pltpu.make_async_remote_copy(
            src_ref=source,
            dst_ref=target,
            send_sem=self.send_sems.at[len(self.copies)],
            recv_sem=self.recv_sems.at[len(self.copies)],
            device_id=peer,
            device_id_type=MESH,
        )
        self.copies.append(copy)
        copy.start()
        return copy


def copies_count(plane, z_size):
    scatter = 1 + (plane - 1) + (z_size - 1)
    return CHUNKS * (2 * scatter + plane - 1) + scatter


def kernel(
    sizes,
    traces_ref, offsets_ref, bins_ref, slots_ref, receivers_ref, band_ref,
    shot_ref, recv_ref,
    traces, corrected, table_t, table, shifts, padded, moved, ahead, parts, fold,
    sums, got_core, acc, got_plane, acc_z, got_z, pilots,
    rsums, rgot_core, racc, rgot_plane, racc_z, rgot_z,
    load_sems, send_sems, recv_sems,
):
    y_size, x_size, z_size = sizes
    plane = y_size * x_size
    shot, cmp = lax.axis_index("shot"), lax.axis_index("cmp")
    core, y, x, z = shot % CORES, shot // CORES, cmp % x_size, cmp // x_size
    q = y * x_size + x
    rows, samples = traces_ref.shape
    bins_count = rows
    chunk = samples // CHUNKS
    taps = band_ref.shape[0]
    held = sums.shape[-2]
    half = LAGS // 2

    def device(core, q, z):
        return ((q // x_size) * CORES + core, z * x_size + q % x_size)

    other = device(1 - core, q, z)
    plane_peers = [device(core, (q + k) % plane, z) for k in range(1, plane)]
    z_peers = [device(core, q, (z + k) % z_size) for k in range(1, z_size)]

    loads = []
    for k in range(CHUNKS):
        columns = pl.ds(k * chunk, chunk)
        loads.append(pltpu.make_async_copy(traces_ref.at[:, columns], traces.at[:, columns], load_sems.at[k]))
        loads[-1].start()
    barrier = pltpu.get_barrier_semaphore()
    peers = [other] + plane_peers + z_peers
    for peer in peers:
        pl.semaphore_signal(barrier, inc=1, device_id=peer, device_id_type=MESH)

    sender = Sender(send_sems, recv_sems)
    shifts[...] = jnp.transpose(jnp.broadcast_to(offsets_ref[...], (LANES, rows)))
    named = (bins_ref[...] == lax.broadcasted_iota(jnp.int32, (bins_count, rows), 0)).astype(jnp.float32)
    table_t[...] = named.astype(jnp.bfloat16)
    table[...] = jnp.transpose(named).astype(jnp.bfloat16)
    traces[:, samples:] = jnp.zeros((rows, LANES), jnp.float32)
    corrected[:, chunk:] = jnp.ones((rows, LANES), jnp.float32)
    padded[:half, :] = jnp.zeros((half, rows), jnp.float32)
    padded[half + samples :, :] = jnp.zeros((half, rows), jnp.float32)

    def width_of(k):
        return chunk + LANES if k == 0 else chunk

    def correct(k):
        first = k * chunk
        loads[k].wait() if k == 0 else None
        if k + 1 < CHUNKS:
            loads[k + 1].wait()
        span = chunk + LANES

        def group(index, carry):
            block = slice(index * GROUP, (index + 1) * GROUP)
            current = traces[block, first : first + span]
            shift = shifts[block, :]
            for level in range(MAXOFF.bit_length()):
                turned = pltpu.roll(current, span - (1 << level), 1)
                chosen = jnp.concatenate([(shift >> level) & 1] * (span // LANES), axis=1) == 1
                current = jnp.where(chosen, turned, current)
            total = jnp.zeros((GROUP, chunk), jnp.float32)
            for tap in range(taps):
                turned = current if tap == 0 else pltpu.roll(current, span - tap, 1)
                total = total + band_ref[tap : tap + 1, first : first + chunk] * turned[:, :chunk]
            corrected[block, :chunk] = total
            return carry

        for index in range(rows // GROUP):
            group(index, 0)
        width = width_of(k)
        result = dot2(table_t[...], corrected[:, :width], ((1,), (0,)))
        if held % 8 == 0:
            sums[k, :, :, :, :, :width] = result.reshape(CORES, plane, z_size, held, width)
        else:
            for block in range(CORES * plane * z_size):
                c_of, rest = divmod(block, plane * z_size)
                sums[k, c_of, rest // z_size, rest % z_size, :, :width] = result[block * held : (block + 1) * held]
        padded[half + first : half + first + chunk, :] = jnp.transpose(corrected[:, :chunk])

    def scatter_core(k):
        lanes = pl.ds(0, width_of(k))
        return [sender.start(sums.at[k, 1 - core, :, :, :, lanes], got_core.at[k, :, :, :, lanes], other)]

    def scatter_plane(k, waits):
        width = width_of(k)
        lanes = pl.ds(0, width)
        waits[0].wait_recv()
        acc[k, :, :, :, :width] = sums[k, core, :, :, :, :width] + got_core[k, :, :, :, :width]
        return [
            sender.start(acc.at[k, (q + j) % plane, :, :, lanes], got_plane.at[k, j - 1, :, :, lanes], plane_peers[j - 1])
            for j in range(1, plane)
        ]

    def scatter_z(k, waits):
        width = width_of(k)
        lanes = pl.ds(0, width)
        total = acc[k, q, :, :, :width]
        for j, copy in enumerate(waits):
            copy.wait_recv()
            total = total + got_plane[k, j, :, :, :width]
        acc_z[k, :, :, :width] = total
        return [
            sender.start(acc_z.at[k, (z + j) % z_size, :, lanes], got_z.at[k, j - 1, :, lanes], z_peers[j - 1])
            for j in range(1, z_size)
        ]

    def gather_z(k, waits):
        width = width_of(k)
        total = acc_z[k, z, :, :width]
        for j, copy in enumerate(waits):
            copy.wait_recv()
            total = total + got_z[k, j, :, :width]
        if k == 0:
            fold[...] = total[:, chunk:]
        pilots[k, core, q, z] = total[:, :chunk] / jnp.concatenate([fold[...]] * (chunk // LANES), axis=1)
        own = pilots.at[k, core, q, z]
        return [sender.start(own, own, peer) for peer in z_peers]

    def gather_plane(k, waits):
        for copy in waits:
            copy.wait_recv()
        own = pilots.at[k, core, q]
        return [sender.start(own, own, peer) for peer in plane_peers] + [sender.start(own, own, other)]

    def gather_core(k, waits):
        across = [waits[-1]]
        for j, copy in enumerate(waits[:-1], 1):
            copy.wait_recv()
            came = pilots.at[k, core, (q + plane - j) % plane]
            across.append(sender.start(came, came, other))
        return across

    def arrive(k, waits):
        for copy in waits:
            copy.wait_recv()
        if held % 8 == 0:
            pilot = pilots[k].reshape(bins_count, chunk)
        else:
            pilot = jnp.concatenate(
                [
                    pilots[k, n // (plane * z_size), n // z_size % plane, n % z_size]
                    for n in range(CORES * plane * z_size)
                ],
                axis=0,
            )
        ahead[k * chunk : (k + 1) * chunk, :] = jnp.transpose(dot2(table[...], pilot, ((1,), (0,))))

    def correlate(first, last):
        lags = LAGS // 8
        steps = 8

        def residue(index, carry):
            for lane in range(0, rows, LANES):
                columns = slice(lane, lane + LANES)

                def step(index_in, totals):
                    base = pl.multiple_of(index_in * (8 * steps), 8 * steps)
                    signal = [ahead[pl.ds(first * chunk + base + 8 * i, 8), columns] for i in range(steps)]
                    shifted = [
                        moved[index, pl.ds(first * chunk + base + 8 * i, 8), columns] for i in range(lags + steps - 1)
                    ]
                    totals = list(totals)
                    for lag in range(lags):
                        terms = [signal[i] * shifted[i + lag] for i in range(steps)]
                        while len(terms) > 1:
                            terms = [terms[i] + terms[i + 1] for i in range(0, len(terms), 2)]
                        totals[lag] = totals[lag] + terms[0]
                    return tuple(totals)

                zero = jnp.zeros((8, LANES), jnp.float32)
                before = tuple(
                    zero if first == 0 else parts[lags - 1 - lag, 7 - index, :, columns] for lag in range(lags)
                )
                totals = lax.fori_loop(0, (last - first) * chunk // (8 * steps), step, before)
                for lag in range(lags):
                    parts[lags - 1 - lag, 7 - index, :, columns] = totals[lag]
            return carry

        for index in range(8):
            residue(index, 0)

    def shift_copies(index):
        moved[index] = padded[index + 1 : index + 1 + moved.shape[1], :]

    stages = [scatter_plane, scatter_z, gather_z, gather_plane, gather_core, arrive]
    waits = [None] * CHUNKS
    fillers = list(range(8))
    for turn in range(CHUNKS + len(stages)):
        if turn < CHUNKS:
            correct(turn)
            if turn == 0:
                pl.semaphore_wait(barrier, len(peers))
            waits[turn] = scatter_core(turn)
        for k in range(CHUNKS):
            stage = turn - k - 1
            if 0 <= stage < len(stages) - 1:
                waits[k] = stages[stage](k, waits[k])
        if turn >= CHUNKS - 1:
            for _ in range(4):
                if fillers:
                    shift_copies(fillers.pop())
        k = turn - len(stages)
        if 0 <= k < CHUNKS:
            while fillers:
                shift_copies(fillers.pop())
            arrive(k, waits[k])
            if (k + 1) % UNIT == 0:
                correlate(k + 1 - UNIT, k + 1)

    corr = (jnp.sum(parts[...], axis=2) * (1.0 / samples)).reshape(LAGS, rows)
    high, low = halves(corr)

    def tabled(ids, count):
        args = dict(dimension_numbers=(((1,), (1,)), ((), ())), preferred_element_type=jnp.float32)
        chosen = (ids == lax.broadcasted_iota(jnp.int32, (count, rows), 0)).astype(jnp.bfloat16)
        return lax.dot_general(chosen, high, **args) + lax.dot_general(chosen, low, **args)

    ids = receivers_ref[...]
    within = ids & (RECV_DEV - 1)
    owner = ids >> log2(RECV_DEV)
    owner_x = owner & (x_size - 1)
    owner_z = (owner >> log2(x_size)) & (z_size - 1)
    owner_core = (owner >> log2(x_size * z_size)) & 1
    owner_y = owner >> log2(x_size * z_size * CORES)
    block = ((owner_core * y_size + owner_y) * x_size + owner_x) * z_size + owner_z
    rsums[...] = tabled(block * RECV_DEV + within, CORES * plane * z_size * RECV_DEV).reshape(rsums.shape)
    first = sender.start(rsums.at[1 - core], rgot_core, other)
    shot_ref[...] = tabled(slots_ref[...], SHOT_DEV)
    first.wait_recv()
    racc[...] = rsums[core] + rgot_core[...]
    waiting = [
        sender.start(racc.at[(q + j) % plane], rgot_plane.at[j - 1], plane_peers[j - 1]) for j in range(1, plane)
    ]
    total = racc[q]
    for j, copy in enumerate(waiting):
        copy.wait_recv()
        total = total + rgot_plane[j]
    racc_z[...] = total
    waiting = [
        sender.start(racc_z.at[(z + j) % z_size], rgot_z.at[j - 1], z_peers[j - 1]) for j in range(1, z_size)
    ]
    total = racc_z[z]
    for j, copy in enumerate(waiting):
        copy.wait_recv()
        total = total + rgot_z[j]
    recv_ref[...] = total
    for copy in sender.copies:
        copy.wait_send()


def local(sizes, traces, offsets, cmp_bin, shot_slot, receiver_id, band):
    rows, samples = traces.shape
    y_size, x_size, z_size = sizes
    plane = y_size * x_size
    held = rows // (CORES * plane * z_size)
    chunk = samples // CHUNKS
    wide = chunk + LANES
    copies = copies_count(plane, z_size)

    def buffer(*shape):
        return pltpu.VMEM(shape, jnp.float32)

    vmem = pl.BlockSpec(memory_space=pltpu.VMEM)
    return pl.pallas_call(
        functools.partial(kernel, sizes),
        out_shape=(
            jax.ShapeDtypeStruct((SHOT_DEV, LAGS), jnp.float32),
            jax.ShapeDtypeStruct((RECV_DEV, LAGS), jnp.float32),
        ),
        in_specs=[pl.BlockSpec(memory_space=pl.ANY)] + [vmem] * 5,
        out_specs=(vmem, vmem),
        scratch_shapes=[
            buffer(rows, samples + LANES),
            buffer(rows, wide),
            pltpu.VMEM((rows, rows), jnp.bfloat16),
            pltpu.VMEM((rows, rows), jnp.bfloat16),
            pltpu.VMEM((rows, LANES), jnp.int32),
            buffer(samples + LAGS, rows),
            buffer(8, samples + LAGS - 8, rows),
            buffer(samples, rows),
            buffer(LAGS // 8, 8, 8, rows),
            buffer(held, LANES),
            buffer(CHUNKS, CORES, plane, z_size, held, wide),
            buffer(CHUNKS, plane, z_size, held, wide),
            buffer(CHUNKS, plane, z_size, held, wide),
            buffer(CHUNKS, plane - 1, z_size, held, wide),
            buffer(CHUNKS, z_size, held, wide),
            buffer(CHUNKS, z_size - 1, held, wide),
            buffer(CHUNKS, CORES, plane, z_size, held, chunk),
            buffer(CORES, plane, z_size, RECV_DEV, LAGS),
            buffer(plane, z_size, RECV_DEV, LAGS),
            buffer(plane, z_size, RECV_DEV, LAGS),
            buffer(plane - 1, z_size, RECV_DEV, LAGS),
            buffer(z_size, RECV_DEV, LAGS),
            buffer(z_size - 1, RECV_DEV, LAGS),
            pltpu.SemaphoreType.DMA((CHUNKS,)),
            pltpu.SemaphoreType.DMA((copies,)),
            pltpu.SemaphoreType.DMA((copies,)),
        ],
        compiler_params=pltpu.CompilerParams(
            collective_id=0, has_side_effects=True, vmem_limit_bytes=VMEM_BYTES
        ),
        name="residual_statics",
    )(
        traces,
        offsets.reshape(1, rows),
        cmp_bin.reshape(1, rows),
        shot_slot.reshape(1, rows),
        receiver_id.reshape(1, rows),
        band,
    )


def solution(mesh):
    shot_size, cmp_size = mesh.shape["shot"], mesh.shape["cmp"]
    z_size = 4 if cmp_size % 8 == 0 else 2
    sizes = (shot_size // CORES, cmp_size // z_size, z_size)
    placed = (
        P(("shot", "cmp"), None),
        P(("shot", "cmp")),
        P(("shot", "cmp"), None),
        P(("shot", "cmp")),
        P(("shot", "cmp")),
        P(),
    )
    return jax.shard_map(
        functools.partial(local, sizes),
        mesh=mesh,
        in_specs=placed,
        out_specs=(P(("shot", "cmp"), None), P(("shot", "cmp"), None)),
        check_vma=False,
    )
```
